32 devices in a mesh: groups: 2 (over y), lon: 4 (over z), lat: 2 (over x), lev: 2 (over core).
Axes of the slice: x: 2, y: 2, z: 4, core: 2. Of those that a mesh axis runs over, the one named last changes fastest.
Arguments:
- state: float32 [4, 60, 64, 512], P('groups', 'lev', 'lat', 'lon'), parts along dimension 0, may hold values from -6 to 6
- winds: float32 [4, 60, 64, 512], P('groups', 'lev', 'lat', 'lon'), parts along dimension 0, may hold values from -0.25 to 0.25
- land_mask: int32 [128, 512], P(('groups', 'lat'), 'lon'), parts along dimension 0, may hold values 0 or 1
- first_weight: bfloat16 [1080, 512], replicated, may hold values from -0.1875 to 0.1875
- second_weight: bfloat16 [512, 512], replicated, may hold values from -0.25 to 0.25
- head_weight: bfloat16 [2, 512, 120], replicated, may hold values from -0.25 to 0.25
Outputs:
- state_next: float32 [4, 60, 64, 512], P('groups', 'lev', 'lat', 'lon'), parts along dimension 0
The draws below stay inside these ranges and needn't reach their ends.
There are 2 independent parts, one for each index of `groups`. The reference program is written for one: setup_inputs(seed, part) draws one part's arguments, and reference() takes and returns one part's arrays. A program takes and returns all parts, laid end to end along the dimension named above; an argument that names none is the same for every part. Nothing has to cross between parts.
All inputs are finite; a program needn't handle non-finite values. No bound on the sum of `land_mask` on one device may be relied on, other than what follows from the above.
Results may differ from the reference program's by a relative error of at most 0.0016.
Values may be sent and summed in bfloat16 or wider, within the bound.
A program may use at most 64 MiB of HBM per device.

```python
import math
import jax
import jax.numpy as jnp
from jax import lax

F = 2
L = 60
HID = 512
STEPS = 4
NLAT = 64
NLON = 512


def touch_ends(drawn, own_key, smallest, top_value):
    extent = drawn.shape
    index_at = [jax.random.randint(jax.random.fold_in(own_key, axis), (), 0, extent[axis]) for axis in range(len(extent))]
    drawn = drawn.at[tuple(index_at)].set(smallest)
    longest = extent.index(max(extent))
    index_at[longest] = (index_at[longest] + 1) % extent[longest]
    return drawn.at[tuple(index_at)].set(top_value)


def shard_levels(rng, shape, split, least, top_value):
    factor_of, own = 1.0, jax.random.fold_in(rng, 6)
    for axis_at, blocks in split:
        draws = jnp.exp(jax.random.uniform(jax.random.fold_in(own, axis_at), (blocks,), jnp.float32, least / len(split), top_value / len(split)))
        factor_of = factor_of * jnp.repeat(draws, shape[axis_at] // blocks).reshape([-1 if axis == axis_at else 1 for axis in range(len(shape))])
    return factor_of


def scatter_about(rng, dims, spread, bound, shards=(), kind=jnp.bfloat16):
    drawn = spread * jax.random.normal(rng, dims, jnp.float32)
    if shards:
        drawn = drawn * shard_levels(rng, dims, shards, -0.22, 0.18)
    return jnp.clip(drawn, -bound, bound).astype(kind)


def setup_inputs(seed: int = 0, part: int = 0) -> dict:
    keys = jax.random.split(jax.random.key(seed), 7)
    own_keys = jax.random.split(jax.random.fold_in(keys[6], part), 7)
    return {
        "state": scatter_about(own_keys[0], (F, L, NLAT, NLON), 1.0, 6.0, ((1, 2), (2, 2), (3, 4)), jnp.float32),
        "winds": jnp.clip(jax.random.uniform(own_keys[1], (2, L, NLAT, NLON), jnp.float32, -0.25, 0.25) * shard_levels(own_keys[1], (2, L, NLAT, NLON), ((1, 2), (2, 2), (3, 4)), -0.4, 0.0), -0.25, 0.25),
        "land_mask": touch_ends((jax.random.randint(own_keys[2], (NLAT, NLON), 0, 3) < 1).astype(jnp.int32), jax.random.fold_in(own_keys[2], 1), 0, 1),
        "first_weight": scatter_about(keys[3], (9 * F * L, HID), (9 * F * L) ** -0.5, 0.1875),
        "second_weight": scatter_about(keys[4], (HID, HID), HID ** -0.5, 0.25),
        "head_weight": scatter_about(keys[5], (2, HID, F * L), HID ** -0.5, 0.25),
    }


def pad_grid(field, width):
    field = jnp.concatenate([field[..., -width:], field, field[..., :width]], axis=-1)
    zero_rows = jnp.zeros(field.shape[:-2] + (width, field.shape[-1]), field.dtype)
    return jnp.concatenate([zero_rows, field, zero_rows], axis=-2)


def substep(tracer, zonal, meridional):
    east = zonal[..., 1:-1, 1:]
    flux_x = jnp.maximum(east, 0.0) * tracer[..., 1:-1, :-1] + jnp.minimum(east, 0.0) * tracer[..., 1:-1, 1:]
    north = meridional[..., 1:, 1:-1]
    flux_y = jnp.maximum(north, 0.0) * tracer[..., :-1, 1:-1] + jnp.minimum(north, 0.0) * tracer[..., 1:, 1:-1]
    return tracer[..., 1:-1, 1:-1] - (flux_x[..., 1:] - flux_x[..., :-1]) - (flux_y[..., 1:, :] - flux_y[..., :-1, :])


def reference(state, winds, land_mask, first_weight, second_weight, head_weight):
    padded_winds = pad_grid(winds, 1)
    zonal = padded_winds[0:1]
    meridional = padded_winds[1:2]
    tracer = state
    for repeat in range(STEPS):
        tracer = substep(pad_grid(tracer, 1), zonal, meridional)
    advected = tracer
    padded_cols = pad_grid(advected.astype(jnp.bfloat16), 1)
    block_rows = math.gcd(NLAT, 8)

    def evaluate(index):
        rows_here = lax.dynamic_slice_in_dim(padded_cols, index * block_rows, block_rows + 2, 2)
        parts = [rows_here[:, :, a:a + block_rows, b:b + NLON] for a in range(3) for b in range(3)]
        features = jnp.stack(parts, 0).reshape(9 * F * L, block_rows * NLON)
        first = jax.nn.silu(lax.dot_general(features, first_weight, (((0,), (0,)), ((), ())), preferred_element_type=jnp.float32)).astype(jnp.bfloat16)
        second = jax.nn.silu(jnp.dot(first, second_weight, preferred_element_type=jnp.float32)).astype(jnp.bfloat16)
        ocean = lax.dot_general(head_weight[0], second, (((0,), (1,)), ((), ())), preferred_element_type=jnp.float32)
        land = lax.dot_general(head_weight[1], second, (((0,), (1,)), ((), ())), preferred_element_type=jnp.float32)
        mask_rows = lax.dynamic_slice_in_dim(land_mask, index * block_rows, block_rows, 0).reshape(1, -1)
        tendency = jnp.where(mask_rows == 1, land, ocean)
        return tendency.reshape(F, L, block_rows, NLON)

    blocks = lax.map(evaluate, jnp.arange(NLAT // block_rows, dtype=jnp.int32))
    tendency = jnp.moveaxis(blocks, 0, 2).reshape(F, L, NLAT, NLON)
    return advected + tendency
```

```python
import jax
import jax.numpy as jnp
from jax import lax
from jax.sharding import PartitionSpec as P

STEPS = 4


def with_halo(cells, sides, width, closed):
    for axis, dim in sides:
        count = lax.axis_size(axis)
        ends = count if closed else count - 1
        head = lax.slice_in_dim(cells, 0, width, axis=dim)
        tail = lax.slice_in_dim(cells, cells.shape[dim] - width, cells.shape[dim], axis=dim)
        cells = jnp.concatenate(
            [
                lax.ppermute(tail, axis, [(i, (i + 1) % count) for i in range(ends)]),
                cells,
                lax.ppermute(head, axis, [((i + 1) % count, i) for i in range(ends)]),
            ],
            axis=dim,
        )
    return cells


def substep(tracer, zonal, meridional):
    east = zonal[..., 1:-1, 1:]
    flux_x = (
        jnp.maximum(east, 0.0) * tracer[..., 1:-1, :-1]
        + jnp.minimum(east, 0.0) * tracer[..., 1:-1, 1:]
    )
    north = meridional[..., 1:, 1:-1]
    flux_y = (
        jnp.maximum(north, 0.0) * tracer[..., :-1, 1:-1]
        + jnp.minimum(north, 0.0) * tracer[..., 1:, 1:-1]
    )
    return (
        tracer[..., 1:-1, 1:-1]
        - (flux_x[..., 1:] - flux_x[..., :-1])
        - (flux_y[..., 1:, :] - flux_y[..., :-1, :])
    )


def neighbourhood(padded, row_count, col_count):
    parts = [padded[:, :, a : a + row_count, b : b + col_count] for a in range(3) for b in range(3)]
    return jnp.stack(parts, 0).reshape(-1, row_count * col_count)


def shards(state, winds, land_mask, first_weight, second_weight, head_weight):
    fields, levels_here, row_count, col_count = state.shape
    deep = STEPS + 1
    both = jnp.concatenate([state, winds], 0)
    both = with_halo(both, (("lon", 3),), deep, True)
    both = with_halo(both, (("lat", 2),), deep, False)
    tracer = both[:fields]
    wind = both[fields:]
    rows_all = row_count * lax.axis_size("lat")
    first_row = lax.axis_index("lat") * row_count
    for repeat in range(STEPS):
        edge = slice(repeat, wind.shape[2] - repeat)
        side = slice(repeat, wind.shape[3] - repeat)
        tracer = substep(tracer, wind[0:1, :, edge, side], wind[1:2, :, edge, side])
        rows = first_row - (deep - repeat - 1) + jnp.arange(tracer.shape[2])
        inside = ((rows >= 0) & (rows < rows_all))[None, None, :, None]
        tracer = jnp.where(inside, tracer, 0.0)
    columns = tracer.astype(jnp.bfloat16)
    tracer = tracer[:, :, 1:-1, 1:-1]
    level_devices = lax.axis_size("lev")
    share = row_count // level_devices
    lev_index = lax.axis_index("lev")
    parts = jnp.stack([columns[:, :, k * share : (k + 1) * share + 2] for k in range(level_devices)], 0)
    got = lax.all_to_all(parts, "lev", split_axis=0, concat_axis=0, tiled=True)
    whole = jnp.moveaxis(got, 0, 1).reshape(fields, level_devices * levels_here, share + 2, -1)
    features = neighbourhood(whole, share, col_count)
    before = lax.dot_general(
        first_weight, features, (((0,), (0,)), ((), ())), preferred_element_type=jnp.float32
    )
    first = jax.nn.silu(before).astype(jnp.bfloat16)
    second = jax.nn.silu(
        lax.dot_general(
            second_weight, first, (((0,), (0,)), ((), ())), preferred_element_type=jnp.float32
        )
    ).astype(jnp.bfloat16)
    ocean = lax.dot_general(
        head_weight[0], second, (((0,), (0,)), ((), ())), preferred_element_type=jnp.float32
    )
    land = lax.dot_general(
        head_weight[1], second, (((0,), (0,)), ((), ())), preferred_element_type=jnp.float32
    )
    mask_rows = lax.dynamic_slice_in_dim(land_mask, lev_index * share, share, 0).reshape(1, -1)
    tendency = jnp.where(mask_rows == 1, land, ocean).reshape(
        fields, levels_here * level_devices, share, col_count
    )
    returned = lax.all_to_all(tendency, "lev", split_axis=1, concat_axis=2, tiled=True)
    return tracer + returned


def solution(mesh):
    placed = (
        P("groups", "lev", "lat", "lon"),
        P("groups", "lev", "lat", "lon"),
        P(("groups", "lat"), "lon"),
        P(),
        P(),
        P(),
    )
    return jax.shard_map(
        shards,
        mesh=mesh,
        in_specs=placed,
        out_specs=P("groups", "lev", "lat", "lon"),
        check_vma=False,
    )
```

```python
import functools

import jax
import jax.numpy as jnp
from jax import lax
from jax.experimental import pallas as pl
from jax.experimental.pallas import tpu as pltpu
from jax.sharding import PartitionSpec as P

STEPS = 4
DEEP = STEPS + 1
LP = 32
PACK = 16
MESH = pl.DeviceIdType.MESH


def silu(v):
    half = 0.5 * v
    return half + half * jnp.tanh(half)


def advance(src, winds, row, keep):
    lanes = winds.shape[2]
    east = winds[row, 2 * LP : 3 * LP, :]
    south = winds[row, 3 * LP : 4 * LP, :]
    north = winds[row + 1, 3 * LP : 4 * LP, :]
    east_p, east_n = jnp.maximum(east, 0.0), jnp.minimum(east, 0.0)
    south_p, south_n = jnp.maximum(south, 0.0), jnp.minimum(south, 0.0)
    north_p, north_n = jnp.maximum(north, 0.0), jnp.minimum(north, 0.0)
    out = []
    for f in range(2):
        levels = slice(f * LP, (f + 1) * LP)
        here = src[row, levels, :]
        below = src[row - 1, levels, :]
        above = src[row + 1, levels, :]
        flux_x = east_p * pltpu.roll(here, 1, 1) + east_n * here
        flux_s = south_p * below + south_n * here
        flux_n = north_p * here + north_n * above
        new = here - (pltpu.roll(flux_x, lanes - 1, 1) - flux_x) - (flux_n - flux_s)
        out.append(new * keep)
    return out


def kernel(
    sizes,
    state_ref, winds_ref, mask_ref, w1_ref, w2_ref, head_ref, out_ref,
    x, y, pack, got, corner, cols, feats, tend, back, w1t, w2t,
    send, recv, tsend, trecv,
):
    levels, rows, lane = sizes
    lon, lat, me = lax.axis_index("lon"), lax.axis_index("lat"), lax.axis_index("lev")
    n_lon, n_lat = lax.axis_size("lon"), lax.axis_size("lat")
    share = rows // 2
    right = {"lon": lax.rem(lon + 1, n_lon)}
    left = {"lon": lax.rem(lon + n_lon - 1, n_lon)}
    north, south = {"lat": lat + 1}, {"lat": lat - 1}
    partner = {"lev": 1 - me}
    has_north, has_south = lat < n_lat - 1, lat > 0

    barrier = pltpu.get_barrier_semaphore()
    for other in (right, left, partner):
        pl.semaphore_signal(barrier, inc=1, device_id=other, device_id_type=MESH)

    @pl.when(has_north)
    def _():
        pl.semaphore_signal(barrier, inc=1, device_id=north, device_id_type=MESH)

    @pl.when(has_south)
    def _():
        pl.semaphore_signal(barrier, inc=1, device_id=south, device_id_type=MESH)

    group = lax.broadcasted_iota(jnp.int32, (4 * LP, lane), 1) // 8

    def fill(g, carry):
        eastward = jnp.zeros((4 * LP, lane), jnp.float32)
        westward = jnp.zeros((4 * LP, lane), jnp.float32)
        for k in range(PACK):
            row = g * PACK + k
            pad = jnp.zeros((8, lane), jnp.float32)
            for f in range(2):
                for part, ref in ((0, state_ref), (2, winds_ref)):
                    base = (part + f) * LP
                    x[DEEP + row, base + LP - 8 : base + LP, 0:lane] = pad
                    x[DEEP + row, base : base + levels, 0:lane] = ref[
                        f, pl.ds(row, levels, stride=rows), :
                    ]
            tile = x[DEEP + row, :, 0:lane]
            eastward = jnp.where(group == k, pltpu.roll(tile, (k * 8 + 8) % lane, 1), eastward)
            westward = jnp.where(group == k, pltpu.roll(tile, k * 8, 1), westward)
        pack[0, g] = eastward
        pack[1, g] = westward
        return carry

    lax.fori_loop(0, rows // PACK, fill, 0)

    peers = 3 + jnp.where(has_north, 1, 0) + jnp.where(has_south, 1, 0)
    pl.semaphore_wait(barrier, peers)

    def remote(src, dst, k, device):
        return pltpu.make_async_remote_copy(
            src_ref=src, dst_ref=dst, send_sem=send.at[k], recv_sem=recv.at[k],
            device_id=device, device_id_type=MESH,
        )

    to_right = remote(pack.at[0], got.at[0], 0, right)
    to_left = remote(pack.at[1], got.at[1], 1, left)
    low, high = pl.ds(0, DEEP), pl.ds(DEEP + rows, DEEP)
    inner = pl.ds(0, lane)
    to_south = remote(
        x.at[pl.ds(DEEP, DEEP), :, inner], x.at[high, :, inner], 2, south
    )
    to_north = remote(
        x.at[pl.ds(rows, DEEP), :, inner], x.at[low, :, inner], 3, north
    )
    corner_south = remote(got.at[:, 0], corner.at[1], 4, south)
    corner_north = remote(got.at[:, rows // PACK - 1], corner.at[0], 5, north)

    to_right.start()
    to_left.start()

    @pl.when(has_south)
    def _():
        to_south.start()

    @pl.when(has_north)
    def _():
        to_north.start()

    ghost = jnp.zeros((DEEP,) + x.shape[1:], jnp.float32)

    @pl.when(jnp.logical_not(has_south))
    def _():
        x[0:DEEP] = ghost

    @pl.when(jnp.logical_not(has_north))
    def _():
        x[DEEP + rows : 2 * DEEP + rows] = ghost

    w1t[...] = w1_ref[...].T
    w2t[...] = w2_ref[...].T

    to_right.wait_recv()
    to_left.wait_recv()

    @pl.when(has_south)
    def _():
        corner_south.start()

    @pl.when(has_north)
    def _():
        corner_north.start()

    near = lax.broadcasted_iota(jnp.int32, (4 * LP, lane), 1) < lane // 2

    def beside(from_left, from_right, k):
        return jnp.where(
            near,
            pltpu.roll(from_right, (lane - k * 8) % lane, 1),
            pltpu.roll(from_left, (2 * lane - 8 - k * 8) % lane, 1),
        )

    def unpack(g, carry):
        for k in range(PACK):
            x[DEEP + g * PACK + k, :, lane : 2 * lane] = beside(got[0, g], got[1, g], k)
        return carry

    lax.fori_loop(0, rows // PACK, unpack, 0)

    @pl.when(has_south)
    def _():
        to_north.wait_recv()
        corner_north.wait_recv()
        for k in range(DEEP):
            x[k, :, lane : 2 * lane] = beside(corner[0, 0], corner[0, 1], PACK - DEEP + k)

    @pl.when(has_north)
    def _():
        to_south.wait_recv()
        corner_south.wait_recv()
        for k in range(DEEP):
            x[DEEP + rows + k, :, lane : 2 * lane] = beside(corner[1, 0], corner[1, 1], k)

    to_right.wait_send()
    to_left.wait_send()

    @pl.when(has_south)
    def _():
        to_south.wait_send()
        corner_south.wait_send()

    @pl.when(has_north)
    def _():
        to_north.wait_send()
        corner_north.wait_send()

    keep_south = jnp.where(has_south, 1.0, 0.0)
    keep_north = jnp.where(has_north, 1.0, 0.0)

    def keep(row):
        return jnp.where(
            row < DEEP, keep_south, jnp.where(row >= DEEP + rows, keep_north, 1.0)
        )

    def substep(src, dst, s):
        def body(row, carry):
            new = advance(src, x, row, keep(row))
            for f in range(2):
                dst[row, f * LP : (f + 1) * LP, :] = new[f]
            return carry

        lax.fori_loop(1 + s, 2 * DEEP + rows - 1 - s, body, 0)

    substep(x, y, 0)
    substep(y, x, 1)
    substep(x, y, 2)

    def last(row, carry):
        new = advance(y, x, row, keep(row))
        for f in range(2):
            at = slice(f * LP, (f + 1) * LP)
            x[row, at, 0:lane] = new[f][:, 0:lane]
            k = row - (DEEP - 1)
            cols[k, 0, at, :] = pltpu.roll(new[f], 1, 1)[:, 0:lane].astype(jnp.bfloat16)
            cols[k, 1, at, :] = new[f][:, 0:lane].astype(jnp.bfloat16)
            cols[k, 2, at, :] = pltpu.roll(new[f], 2 * lane - 1, 1)[:, 0:lane].astype(jnp.bfloat16)
        return carry

    lax.fori_loop(DEEP - 1, DEEP + rows + 1, last, 0)

    mine = pl.ds(me * share, share + 2)
    theirs = pl.ds((1 - me) * share, share + 2)
    half = pl.ds(me * 2 * LP, 2 * LP)
    over = remote(cols.at[theirs], feats.at[:, :, half], 6, partner)
    over.start()
    own = pltpu.make_async_copy(cols.at[mine], feats.at[:, :, half], send.at[7])
    own.start()
    own.wait()
    over.wait_recv()

    batch = 4
    steps = share // batch

    def returned(g):
        return pltpu.make_async_remote_copy(
            src_ref=tend.at[pl.ds(g * batch, batch), pl.ds((1 - me) * 2 * LP, 2 * LP)],
            dst_ref=back.at[pl.ds(g * batch, batch)],
            send_sem=tsend.at[g], recv_sem=trecv.at[g], device_id=partner, device_id_type=MESH,
        )

    def emit(row, tendency):
        for f in range(2):
            at = slice(f * LP, f * LP + levels)
            out_ref[f, pl.ds(row, levels, stride=rows), :] = (
                x[DEEP + row, at, 0:lane] + tendency[at]
            )

    def physics(g, carry):
        features = jnp.concatenate(
            [
                feats[pl.ds(g * batch + k, 3)].reshape(9 * 4 * LP, lane)
                for k in range(batch)
            ],
            axis=1,
        )
        first = silu(
            jnp.dot(w1t[...], features, preferred_element_type=jnp.float32)
        ).astype(jnp.bfloat16)
        second = silu(
            jnp.dot(w2t[...], first, preferred_element_type=jnp.float32)
        ).astype(jnp.bfloat16)
        both = jnp.dot(head_ref[...], second, preferred_element_type=jnp.float32)
        for k in range(batch):
            row = g * batch + k
            land = mask_ref[pl.ds(me * share + row, 1), :] == 1
            at = slice(k * lane, (k + 1) * lane)
            tend[row] = jnp.where(land, both[4 * LP :, at], both[: 4 * LP, at])
        returned(g).start()
        for k in range(batch):
            row = g * batch + k
            emit(me * share + row, tend[row, half])
        return carry

    lax.fori_loop(0, steps, physics, 0)

    def finish(g, carry):
        returned(g).wait_recv()
        for k in range(batch):
            row = g * batch + k
            emit((1 - me) * share + row, back[row])
        return carry

    lax.fori_loop(0, steps, finish, 0)
    over.wait_send()

    def drain(g, carry):
        returned(g).wait_send()
        return carry

    lax.fori_loop(0, steps, drain, 0)


def shards(state, winds, land_mask, first_weight, second_weight, head_weight):
    fields, levels, rows, lane = state.shape
    width = second_weight.shape[0]
    lev = lax.axis_size("lev")
    spare = LP - levels
    w1 = first_weight.reshape(9, fields, lev, levels, width).transpose(0, 2, 1, 3, 4)
    w1 = jnp.pad(w1, ((0, 0),) * 3 + ((0, spare), (0, 0))).reshape(-1, width)
    head = head_weight.transpose(0, 2, 1).reshape(2, fields, lev, levels, width)
    head = head.transpose(0, 2, 1, 3, 4)
    head = jnp.pad(head, ((0, 0),) * 3 + ((0, spare), (0, 0))).reshape(-1, width)
    inside = pl.BlockSpec(memory_space=pltpu.VMEM)
    f32, bf16 = jnp.float32, jnp.bfloat16
    groups = rows // PACK
    share = rows // 2
    out = pl.pallas_call(
        functools.partial(kernel, (levels, rows, lane)),
        out_shape=jax.ShapeDtypeStruct((fields, levels * rows, lane), f32),
        in_specs=[inside] * 6,
        out_specs=inside,
        scratch_shapes=[
            pltpu.VMEM((rows + 2 * DEEP, 4 * LP, 2 * lane), f32),
            pltpu.VMEM((rows + 2 * DEEP, 2 * LP, 2 * lane), f32),
            pltpu.VMEM((2, groups, 4 * LP, lane), f32),
            pltpu.VMEM((2, groups, 4 * LP, lane), f32),
            pltpu.VMEM((2, 2, 4 * LP, lane), f32),
            pltpu.VMEM((rows + 2, 3, 2 * LP, lane), bf16),
            pltpu.VMEM((share + 2, 3, 4 * LP, lane), bf16),
            pltpu.VMEM((share, 4 * LP, lane), f32),
            pltpu.VMEM((share, 2 * LP, lane), f32),
            pltpu.VMEM((width, 9 * 4 * LP), bf16),
            pltpu.VMEM((width, width), bf16),
            pltpu.SemaphoreType.DMA((8,)),
            pltpu.SemaphoreType.DMA((8,)),
            pltpu.SemaphoreType.DMA((share // 4,)),
            pltpu.SemaphoreType.DMA((share // 4,)),
        ],
        compiler_params=pltpu.CompilerParams(
            collective_id=0, has_side_effects=True, vmem_limit_bytes=48 * 1024 * 1024
        ),
    )(
        state.reshape(fields, levels * rows, lane),
        winds.reshape(2, levels * rows, lane),
        land_mask,
        w1,
        second_weight,
        head,
    )
    return out.reshape(state.shape)


def solution(mesh):
    placed = (
        P("groups", "lev", "lat", "lon"),
        P("groups", "lev", "lat", "lon"),
        P(("groups", "lat"), "lon"),
        P(),
        P(),
        P(),
    )
    return jax.shard_map(
        shards,
        mesh=mesh,
        in_specs=placed,
        out_specs=P("groups", "lev", "lat", "lon"),
        check_vma=False,
    )
```

```python
import functools

import jax
import jax.numpy as jnp
from jax import lax
from jax.experimental import pallas as pl
from jax.experimental.pallas import tpu as pltpu
from jax.sharding import PartitionSpec as P

STEPS = 4
DEEP = STEPS + 1
LP = 32
EDGE = 8
MESH = pl.DeviceIdType.MESH


def silu(v):
    half = 0.5 * v
    return half + half * jnp.tanh(half)


def chunks():
    for c in range(LP // 8):
        yield 8 * c, LP + 8 * c, (8 * c, LP + 8 * c)
    for side in range(2):
        yield 2 * LP + 8 * side, 2 * LP + 16 + 8 * side, (2 * LP + 8 * side,)


def advance(src, winds, row, keeps):
    n = len(keeps)
    for z_at, m_at, tracers in chunks():
        zonal = [winds[row + k, z_at : z_at + 8, :] for k in range(n)]
        merid = [winds[row + k, m_at : m_at + 8, :] for k in range(n + 1)]
        for at in tracers:
            cells = [src[row - 1 + k, at : at + 8, :] for k in range(n + 2)]
            flux_y = [
                merid[k] * jnp.where(merid[k] > 0.0, cells[k], cells[k + 1])
                for k in range(n + 1)
            ]
            for k in range(n):
                here = cells[k + 1]
                lanes = here.shape[1]
                flux_x = zonal[k] * jnp.where(zonal[k] > 0.0, pltpu.roll(here, 1, 1), here)
                new = here - (pltpu.roll(flux_x, lanes - 1, 1) - flux_x)
                new = new - (flux_y[k + 1] - flux_y[k])
                yield k, at, new * keeps[k]


def kernel(
    sizes,
    state_ref, winds_ref, mask_ref, w1_ref, w2_ref, head_ref, out_ref,
    x, y, w, pack, got, cols, feats, tend, back, w1t, w2t,
    send, recv, tsend, trecv,
):
    levels, rows, lane = sizes
    lon, lat, me = lax.axis_index("lon"), lax.axis_index("lat"), lax.axis_index("lev")
    n_lon, n_lat = lax.axis_size("lon"), lax.axis_size("lat")
    share = rows // 2
    right = {"lon": lax.rem(lon + 1, n_lon)}
    left = {"lon": lax.rem(lon + n_lon - 1, n_lon)}
    north, south = {"lat": lat + 1}, {"lat": lat - 1}
    partner = {"lev": 1 - me}
    has_north, has_south = lat < n_lat - 1, lat > 0

    barrier = pltpu.get_barrier_semaphore()
    for other in (right, left, partner):
        pl.semaphore_signal(barrier, inc=1, device_id=other, device_id_type=MESH)

    @pl.when(has_north)
    def _():
        pl.semaphore_signal(barrier, inc=1, device_id=north, device_id_type=MESH)

    @pl.when(has_south)
    def _():
        pl.semaphore_signal(barrier, inc=1, device_id=south, device_id_type=MESH)

    place = lax.broadcasted_iota(jnp.int32, (8, lane), 1)
    group = place // (2 * EDGE)
    first_half = place % (2 * EDGE) < EDGE

    def fill(row, carry):
        pad = jnp.zeros((8, lane), jnp.float32)
        for f in range(2):
            for into, ref in ((x, state_ref), (w, winds_ref)):
                base = f * LP
                into[DEEP + row, base + LP - 8 : base + LP, :] = pad
                into[DEEP + row, base : base + levels, :] = ref[
                    f, pl.ds(row, levels, stride=rows), :
                ]
        for side in range(2):
            begin = lane - EDGE if side == 0 else 0
            halves = []
            for into, half_at in ((x, 0), (w, EDGE)):
                acc = pad
                for c in range(8):
                    tile = into[DEEP + row, 8 * c : 8 * c + 8, :]
                    shift = (c * 2 * EDGE + half_at - begin) % lane
                    moved = pltpu.roll(tile, shift, 1) if shift else tile
                    acc = jnp.where(group == c, moved, acc)
                halves.append(acc)
            pack[side, DEEP + row] = jnp.where(first_half, halves[0], halves[1])
        return carry

    lax.fori_loop(0, rows, fill, 0)

    peers = 3 + jnp.where(has_north, 1, 0) + jnp.where(has_south, 1, 0)
    pl.semaphore_wait(barrier, peers)

    def remote(src, dst, k, device):
        return pltpu.make_async_remote_copy(
            src_ref=src, dst_ref=dst, send_sem=send.at[k], recv_sem=recv.at[k],
            device_id=device, device_id_type=MESH,
        )

    interior = pl.ds(DEEP, rows)
    to_right = remote(pack.at[0, interior], got.at[0, interior], 0, right)
    to_left = remote(pack.at[1, interior], got.at[1, interior], 1, left)
    low, high = pl.ds(0, DEEP), pl.ds(DEEP + rows, DEEP)
    bottom, top = pl.ds(DEEP, DEEP), pl.ds(rows, DEEP)
    main = pl.ds(0, 2 * LP)
    to_south = [
        remote(x.at[bottom, main], x.at[high, main], 2, south),
        remote(w.at[bottom, main], w.at[high, main], 3, south),
        remote(pack.at[:, bottom], pack.at[:, high], 4, south),
    ]
    to_north = [
        remote(x.at[top, main], x.at[low, main], 6, north),
        remote(w.at[top, main], w.at[low, main], 7, north),
        remote(pack.at[:, top], pack.at[:, low], 8, north),
    ]
    corner_south = remote(got.at[:, bottom], got.at[:, high], 5, south)
    corner_north = remote(got.at[:, top], got.at[:, low], 9, north)

    to_right.start()
    to_left.start()

    @pl.when(has_south)
    def _():
        for copy in to_south:
            copy.start()

    @pl.when(has_north)
    def _():
        for copy in to_north:
            copy.start()

    def clear(begin):
        for k in range(DEEP):
            x[begin + k] = jnp.zeros(x.shape[1:], jnp.float32)
            w[begin + k] = jnp.zeros(w.shape[1:], jnp.float32)
            for side in range(2):
                pack[side, begin + k] = jnp.zeros((8, lane), jnp.float32)
                got[side, begin + k] = jnp.zeros((8, lane), jnp.float32)

    @pl.when(jnp.logical_not(has_south))
    def _():
        clear(0)

    @pl.when(jnp.logical_not(has_north))
    def _():
        clear(DEEP + rows)

    w1t[...] = w1_ref[...].T
    w2t[...] = w2_ref[...].T

    to_right.wait_recv()
    to_left.wait_recv()

    @pl.when(has_south)
    def _():
        corner_south.start()

    @pl.when(has_north)
    def _():
        corner_north.start()

    def strips(row, carry):
        for side in range(2):
            if side == 0:
                outer, inner = got[0, row], pack[1, row]
            else:
                outer, inner = pack[0, row], got[1, row]
            tracer = jnp.where(first_half, outer, pltpu.roll(inner, EDGE, 1))
            wind = jnp.where(first_half, pltpu.roll(outer, lane - EDGE, 1), inner)
            swapped = pltpu.roll(wind, lane // 2, 1)
            at = 2 * LP + 8 * side
            x[row, at : at + 8, :] = tracer
            w[row, at : at + 8, :] = jnp.where(place < lane // 2, wind, swapped)
            w[row, at + 16 : at + 24, :] = jnp.where(place < lane // 2, swapped, wind)
        return carry

    lax.fori_loop(DEEP, DEEP + rows, strips, 0)

    @pl.when(has_south)
    def _():
        for copy in to_north:
            copy.wait_recv()
        corner_north.wait_recv()

    @pl.when(has_north)
    def _():
        for copy in to_south:
            copy.wait_recv()
        corner_south.wait_recv()

    lax.fori_loop(0, DEEP, strips, 0)
    lax.fori_loop(DEEP + rows, 2 * DEEP + rows, strips, 0)

    to_right.wait_send()
    to_left.wait_send()

    @pl.when(has_south)
    def _():
        for copy in to_south:
            copy.wait_send()
        corner_south.wait_send()

    @pl.when(has_north)
    def _():
        for copy in to_north:
            copy.wait_send()
        corner_north.wait_send()

    keep_south = jnp.where(has_south, 1.0, 0.0)
    keep_north = jnp.where(has_north, 1.0, 0.0)

    def keep(row):
        return jnp.where(
            row < DEEP, keep_south, jnp.where(row >= DEEP + rows, keep_north, 1.0)
        )

    def substep(src, dst, s):
        first = 1 + s
        count = 2 * DEEP + rows - 2 - 2 * s

        def body(i, carry):
            row = first + 2 * i
            for k, at, new in advance(src, w, row, [keep(row), keep(row + 1)]):
                dst[row + k, at : at + 8, :] = new
            return carry

        lax.fori_loop(0, count // 2, body, 0)

    substep(x, y, 0)
    substep(y, x, 1)
    substep(x, y, 2)
    substep(y, x, 3)

    def merge(k, carry):
        row = k + DEEP - 1
        west = x[row, 2 * LP : 2 * LP + 8, :]
        east = x[row, 2 * LP + 8 : 2 * LP + 16, :]
        for c in range(0, 8, 2):
            shifted = ([], [], [])
            for d in (c, c + 1):
                at = slice(8 * d, 8 * d + 8)
                from_west = pltpu.roll(west, (2 * lane - EDGE - d * 2 * EDGE) % lane, 1)
                shift = (lane - EDGE - d * 2 * EDGE) % lane
                from_east = pltpu.roll(east, shift, 1) if shift else east
                cells = jnp.where(place < STEPS, from_west, x[row, at, :])
                cells = jnp.where(place >= lane - STEPS, from_east, cells)
                x[row, at, :] = cells
                shifted[0].append(
                    pltpu.roll(jnp.where(place == lane - 1, from_west, cells), 1, 1)
                )
                shifted[1].append(cells)
                shifted[2].append(
                    pltpu.roll(jnp.where(place == 0, from_east, cells), lane - 1, 1)
                )
            for b in range(3):
                cols[k, b, 8 * c : 8 * c + 16, :] = jnp.concatenate(shifted[b], 0).astype(
                    jnp.bfloat16
                )
        return carry

    lax.fori_loop(0, rows + 2, merge, 0)

    mine = pl.ds(me * share, share + 2)
    theirs = pl.ds((1 - me) * share, share + 2)
    half = pl.ds(me * 2 * LP, 2 * LP)
    over = remote(cols.at[theirs], feats.at[:, :, half], 10, partner)
    over.start()
    own = pltpu.make_async_copy(cols.at[mine], feats.at[:, :, half], send.at[11])
    own.start()
    own.wait()
    over.wait_recv()

    batch = 4
    steps = share // batch

    def returned(g):
        return pltpu.make_async_remote_copy(
            src_ref=tend.at[pl.ds(g * batch, batch), pl.ds((1 - me) * 2 * LP, 2 * LP)],
            dst_ref=back.at[pl.ds(g * batch, batch)],
            send_sem=tsend.at[g], recv_sem=trecv.at[g], device_id=partner, device_id_type=MESH,
        )

    def emit(row, tendency):
        for f in range(2):
            at = slice(f * LP, f * LP + levels)
            out_ref[f, pl.ds(row, levels, stride=rows), :] = (
                x[DEEP + row, at, :] + tendency[at]
            )

    def physics(g, carry):
        features = jnp.concatenate(
            [
                feats[pl.ds(g * batch + k, 3)].reshape(9 * 4 * LP, lane)
                for k in range(batch)
            ],
            axis=1,
        )
        first = silu(
            jnp.dot(w1t[...], features, preferred_element_type=jnp.float32)
        ).astype(jnp.bfloat16)
        second = silu(
            jnp.dot(w2t[...], first, preferred_element_type=jnp.float32)
        ).astype(jnp.bfloat16)
        both = jnp.dot(head_ref[...], second, preferred_element_type=jnp.float32)
        for k in range(batch):
            row = g * batch + k
            land = mask_ref[pl.ds(me * share + row, 1), :] == 1
            at = slice(k * lane, (k + 1) * lane)
            tend[row] = jnp.where(land, both[4 * LP :, at], both[: 4 * LP, at])
        returned(g).start()
        for k in range(batch):
            row = g * batch + k
            emit(me * share + row, tend[row, half])
        return carry

    lax.fori_loop(0, steps, physics, 0)

    def finish(g, carry):
        returned(g).wait_recv()
        for k in range(batch):
            row = g * batch + k
            emit((1 - me) * share + row, back[row])
        return carry

    lax.fori_loop(0, steps, finish, 0)
    over.wait_send()

    def drain(g, carry):
        returned(g).wait_send()
        return carry

    lax.fori_loop(0, steps, drain, 0)


def shards(state, winds, land_mask, first_weight, second_weight, head_weight):
    fields, levels, rows, lane = state.shape
    width = second_weight.shape[0]
    lev = lax.axis_size("lev")
    spare = LP - levels
    w1 = first_weight.reshape(9, fields, lev, levels, width).transpose(0, 2, 1, 3, 4)
    w1 = jnp.pad(w1, ((0, 0),) * 3 + ((0, spare), (0, 0))).reshape(-1, width)
    head = head_weight.transpose(0, 2, 1).reshape(2, fields, lev, levels, width)
    head = head.transpose(0, 2, 1, 3, 4)
    head = jnp.pad(head, ((0, 0),) * 3 + ((0, spare), (0, 0))).reshape(-1, width)
    inside = pl.BlockSpec(memory_space=pltpu.VMEM)
    f32, bf16 = jnp.float32, jnp.bfloat16
    share = rows // 2
    out = pl.pallas_call(
        functools.partial(kernel, (levels, rows, lane)),
        out_shape=jax.ShapeDtypeStruct((fields, levels * rows, lane), f32),
        in_specs=[inside] * 6,
        out_specs=inside,
        scratch_shapes=[
            pltpu.VMEM((rows + 2 * DEEP, 2 * LP + 16, lane), f32),
            pltpu.VMEM((rows + 2 * DEEP, 2 * LP + 16, lane), f32),
            pltpu.VMEM((rows + 2 * DEEP, 2 * LP + 32, lane), f32),
            pltpu.VMEM((2, rows + 2 * DEEP, 8, lane), f32),
            pltpu.VMEM((2, rows + 2 * DEEP, 8, lane), f32),
            pltpu.VMEM((rows + 2, 3, 2 * LP, lane), bf16),
            pltpu.VMEM((share + 2, 3, 4 * LP, lane), bf16),
            pltpu.VMEM((share, 4 * LP, lane), f32),
            pltpu.VMEM((share, 2 * LP, lane), f32),
            pltpu.VMEM((width, 9 * 4 * LP), bf16),
            pltpu.VMEM((width, width), bf16),
            pltpu.SemaphoreType.DMA((12,)),
            pltpu.SemaphoreType.DMA((12,)),
            pltpu.SemaphoreType.DMA((share // 4,)),
            pltpu.SemaphoreType.DMA((share // 4,)),
        ],
        compiler_params=pltpu.CompilerParams(
            collective_id=0, has_side_effects=True, vmem_limit_bytes=48 * 1024 * 1024
        ),
    )(
        state.reshape(fields, levels * rows, lane),
        winds.reshape(2, levels * rows, lane),
        land_mask,
        w1,
        second_weight,
        head,
    )
    return out.reshape(state.shape)


def solution(mesh):
    placed = (
        P("groups", "lev", "lat", "lon"),
        P("groups", "lev", "lat", "lon"),
        P(("groups", "lat"), "lon"),
        P(),
        P(),
        P(),
    )
    return jax.shard_map(
        shards,
        mesh=mesh,
        in_specs=placed,
        out_specs=P("groups", "lev", "lat", "lon"),
        check_vma=False,
    )
```

```python
import functools

import jax
import jax.numpy as jnp
from jax import lax
from jax.experimental import pallas as pl
from jax.experimental.pallas import tpu as pltpu
from jax.sharding import PartitionSpec as P

STEPS = 4
DEEP = STEPS + 1
LP = 32
EDGE = 8
MESH = pl.DeviceIdType.MESH


def silu(v):
    half = 0.5 * v
    return half + half * jnp.tanh(half)


def chunks():
    for c in range(LP // 8):
        yield 8 * c, LP + 8 * c, (8 * c, LP + 8 * c)
    for side in range(2):
        yield 2 * LP + 8 * side, 2 * LP + 16 + 8 * side, (2 * LP + 8 * side,)


def advance(src, winds, row, keeps):
    n = len(keeps)
    for z_at, m_at, tracers in chunks():
        zonal = [winds[row + k, z_at : z_at + 8, :] for k in range(n)]
        merid = [winds[row + k, m_at : m_at + 8, :] for k in range(n + 1)]
        for at in tracers:
            cells = [src[row - 1 + k, at : at + 8, :] for k in range(n + 2)]
            flux_y = [
                merid[k] * jnp.where(merid[k] > 0.0, cells[k], cells[k + 1])
                for k in range(n + 1)
            ]
            for k in range(n):
                here = cells[k + 1]
                lanes = here.shape[1]
                flux_x = zonal[k] * jnp.where(zonal[k] > 0.0, pltpu.roll(here, 1, 1), here)
                new = here - (pltpu.roll(flux_x, lanes - 1, 1) - flux_x)
                new = new - (flux_y[k + 1] - flux_y[k])
                yield k, at, new * keeps[k]


def kernel(
    sizes,
    state_ref, winds_ref, mask_ref, w1_ref, w2_ref, head_ref, out_ref,
    x, y, w, pack, got, cols, feats, tend, back, w1t, w2t,
    send, recv, tsend, trecv,
):
    levels, rows, lane = sizes
    lon, lat, me = lax.axis_index("lon"), lax.axis_index("lat"), lax.axis_index("lev")
    n_lon, n_lat = lax.axis_size("lon"), lax.axis_size("lat")
    share = rows // 2
    right = {"lon": lax.rem(lon + 1, n_lon)}
    left = {"lon": lax.rem(lon + n_lon - 1, n_lon)}
    north, south = {"lat": lat + 1}, {"lat": lat - 1}
    partner = {"lev": 1 - me}
    has_north, has_south = lat < n_lat - 1, lat > 0

    barrier = pltpu.get_barrier_semaphore()
    for other in (right, left, partner):
        pl.semaphore_signal(barrier, inc=1, device_id=other, device_id_type=MESH)

    @pl.when(has_north)
    def _():
        pl.semaphore_signal(barrier, inc=1, device_id=north, device_id_type=MESH)

    @pl.when(has_south)
    def _():
        pl.semaphore_signal(barrier, inc=1, device_id=south, device_id_type=MESH)

    place = lax.broadcasted_iota(jnp.int32, (8, lane), 1)
    group = place // (2 * EDGE)
    first_half = place % (2 * EDGE) < EDGE

    def tiles(ref, row):
        for f in range(2):
            for c in range(LP // 8):
                count = min(8, levels - 8 * c)
                tile = ref[f, pl.ds(row + 8 * c * rows, count, stride=rows), :]
                if count < 8:
                    tile = jnp.concatenate([tile, jnp.zeros((8 - count, lane), jnp.float32)], 0)
                yield tile

    def fill_row(row):
        tracers, winds = list(tiles(state_ref, row)), list(tiles(winds_ref, row))
        for into, values in ((x, tracers), (w, winds)):
            for c, tile in enumerate(values):
                into[DEEP + row, 8 * c : 8 * c + 8, :] = tile
        for side in range(2):
            begin = lane - EDGE if side == 0 else 0
            halves = []
            for values, half_at in ((tracers, 0), (winds, EDGE)):
                acc = jnp.zeros((8, lane), jnp.float32)
                for c, tile in enumerate(values):
                    shift = (c * 2 * EDGE + half_at - begin) % lane
                    moved = pltpu.roll(tile, shift, 1) if shift else tile
                    acc = jnp.where(group == c, moved, acc)
                halves.append(acc)
            pack[side, DEEP + row] = jnp.where(first_half, halves[0], halves[1])

    def fill(i, carry):
        fill_row(2 * i)
        fill_row(2 * i + 1)
        return carry

    lax.fori_loop(0, rows // 2, fill, 0)

    peers = 3 + jnp.where(has_north, 1, 0) + jnp.where(has_south, 1, 0)
    pl.semaphore_wait(barrier, peers)

    def remote(src, dst, k, device):
        return pltpu.make_async_remote_copy(
            src_ref=src, dst_ref=dst, send_sem=send.at[k], recv_sem=recv.at[k],
            device_id=device, device_id_type=MESH,
        )

    interior = pl.ds(DEEP, rows)
    to_right = remote(pack.at[0, interior], got.at[0, interior], 0, right)
    to_left = remote(pack.at[1, interior], got.at[1, interior], 1, left)
    low, high = pl.ds(0, DEEP), pl.ds(DEEP + rows, DEEP)
    bottom, top = pl.ds(DEEP, DEEP), pl.ds(rows, DEEP)
    main = pl.ds(0, 2 * LP)
    to_south = [
        remote(x.at[bottom, main], x.at[high, main], 2, south),
        remote(w.at[bottom, main], w.at[high, main], 3, south),
        remote(pack.at[:, bottom], pack.at[:, high], 4, south),
    ]
    to_north = [
        remote(x.at[top, main], x.at[low, main], 6, north),
        remote(w.at[top, main], w.at[low, main], 7, north),
        remote(pack.at[:, top], pack.at[:, low], 8, north),
    ]
    corner_south = remote(got.at[:, bottom], got.at[:, high], 5, south)
    corner_north = remote(got.at[:, top], got.at[:, low], 9, north)

    to_right.start()
    to_left.start()

    @pl.when(has_south)
    def _():
        for copy in to_south:
            copy.start()

    @pl.when(has_north)
    def _():
        for copy in to_north:
            copy.start()

    def clear(begin):
        for k in range(DEEP):
            x[begin + k] = jnp.zeros(x.shape[1:], jnp.float32)
            w[begin + k] = jnp.zeros(w.shape[1:], jnp.float32)
            for side in range(2):
                pack[side, begin + k] = jnp.zeros((8, lane), jnp.float32)
                got[side, begin + k] = jnp.zeros((8, lane), jnp.float32)

    @pl.when(jnp.logical_not(has_south))
    def _():
        clear(0)

    @pl.when(jnp.logical_not(has_north))
    def _():
        clear(DEEP + rows)

    w1t[...] = w1_ref[...].T
    w2t[...] = w2_ref[...].T

    to_right.wait_recv()
    to_left.wait_recv()

    @pl.when(has_south)
    def _():
        corner_south.start()

    @pl.when(has_north)
    def _():
        corner_north.start()

    def strips(row, carry):
        for side in range(2):
            if side == 0:
                outer, inner = got[0, row], pack[1, row]
            else:
                outer, inner = pack[0, row], got[1, row]
            tracer = jnp.where(first_half, outer, pltpu.roll(inner, EDGE, 1))
            wind = jnp.where(first_half, pltpu.roll(outer, lane - EDGE, 1), inner)
            swapped = pltpu.roll(wind, lane // 2, 1)
            at = 2 * LP + 8 * side
            x[row, at : at + 8, :] = tracer
            w[row, at : at + 8, :] = jnp.where(place < lane // 2, wind, swapped)
            w[row, at + 16 : at + 24, :] = jnp.where(place < lane // 2, swapped, wind)
        return carry

    def strips_four(i, carry):
        for k in range(4):
            strips(DEEP + 4 * i + k, carry)
        return carry

    lax.fori_loop(0, rows // 4, strips_four, 0)

    @pl.when(has_south)
    def _():
        for copy in to_north:
            copy.wait_recv()
        corner_north.wait_recv()

    @pl.when(has_north)
    def _():
        for copy in to_south:
            copy.wait_recv()
        corner_south.wait_recv()

    def strips_ends(k, carry):
        strips(k, carry)
        strips(DEEP + rows + k, carry)
        return carry

    lax.fori_loop(0, DEEP, strips_ends, 0)

    to_right.wait_send()
    to_left.wait_send()

    @pl.when(has_south)
    def _():
        for copy in to_south:
            copy.wait_send()
        corner_south.wait_send()

    @pl.when(has_north)
    def _():
        for copy in to_north:
            copy.wait_send()
        corner_north.wait_send()

    keep_south = jnp.where(has_south, 1.0, 0.0)
    keep_north = jnp.where(has_north, 1.0, 0.0)

    def keep(row):
        return jnp.where(
            row < DEEP, keep_south, jnp.where(row >= DEEP + rows, keep_north, 1.0)
        )

    def substep(src, dst, s):
        first = 1 + s // 2 * 2
        count = 2 * DEEP + rows + 1 - 2 * first - 1

        def body(i, carry):
            row = first + 4 * i
            for k, at, new in advance(src, w, row, [keep(row + k) for k in range(4)]):
                dst[row + k, at : at + 8, :] = new
            return carry

        lax.fori_loop(0, count // 4, body, 0)

    substep(x, y, 0)
    substep(y, x, 1)
    substep(x, y, 2)
    substep(y, x, 3)

    def merge_row(k):
        row = k + DEEP - 1
        west = x[row, 2 * LP : 2 * LP + 8, :]
        east = x[row, 2 * LP + 8 : 2 * LP + 16, :]
        for c in range(0, 8, 2):
            shifted = ([], [], [])
            for d in (c, c + 1):
                at = slice(8 * d, 8 * d + 8)
                from_west = pltpu.roll(west, (2 * lane - EDGE - d * 2 * EDGE) % lane, 1)
                shift = (lane - EDGE - d * 2 * EDGE) % lane
                from_east = pltpu.roll(east, shift, 1) if shift else east
                cells = jnp.where(place < STEPS, from_west, x[row, at, :])
                cells = jnp.where(place >= lane - STEPS, from_east, cells)
                y[row, at, :] = cells
                shifted[0].append(
                    pltpu.roll(jnp.where(place == lane - 1, from_west, cells), 1, 1)
                )
                shifted[1].append(cells)
                shifted[2].append(
                    pltpu.roll(jnp.where(place == 0, from_east, cells), lane - 1, 1)
                )
            for b in range(3):
                cols[k, b, 8 * c : 8 * c + 16, :] = jnp.concatenate(shifted[b], 0).astype(
                    jnp.bfloat16
                )

    def merge_from(start, count):
        def body(i, carry):
            merge_row(start + 2 * i)
            merge_row(start + 2 * i + 1)
            return carry

        lax.fori_loop(0, count // 2, body, 0)

    mine = pl.ds(me * share, share + 2)
    theirs = pl.ds((1 - me) * share, share + 2)
    half = pl.ds(me * 2 * LP, 2 * LP)
    over = remote(cols.at[theirs], feats.at[:, :, half], 10, partner)
    merge_from((1 - me) * share, share + 2)
    over.start()
    merge_from(me * (share + 2), share)
    own = pltpu.make_async_copy(cols.at[mine], feats.at[:, :, half], send.at[11])
    own.start()
    own.wait()
    over.wait_recv()

    batch = 4
    steps = share // batch

    def returned(g):
        return pltpu.make_async_remote_copy(
            src_ref=tend.at[pl.ds(g * batch, batch), pl.ds((1 - me) * 2 * LP, 2 * LP)],
            dst_ref=back.at[pl.ds(g * batch, batch)],
            send_sem=tsend.at[g], recv_sem=trecv.at[g], device_id=partner, device_id_type=MESH,
        )

    def emit(row, tendency):
        for f in range(2):
            at = slice(f * LP, f * LP + levels)
            out_ref[f, pl.ds(row, levels, stride=rows), :] = (
                y[DEEP + row, at, :] + tendency[at]
            )

    def physics(g, carry):
        features = jnp.concatenate(
            [
                feats[pl.ds(g * batch + k, 3)].reshape(9 * 4 * LP, lane)
                for k in range(batch)
            ],
            axis=1,
        )
        first = silu(
            jnp.dot(w1t[...], features, preferred_element_type=jnp.float32)
        ).astype(jnp.bfloat16)
        second = silu(
            jnp.dot(w2t[...], first, preferred_element_type=jnp.float32)
        ).astype(jnp.bfloat16)
        both = jnp.dot(head_ref[...], second, preferred_element_type=jnp.float32)
        for k in range(batch):
            row = g * batch + k
            land = mask_ref[pl.ds(me * share + row, 1), :] == 1
            at = slice(k * lane, (k + 1) * lane)
            tend[row] = jnp.where(land, both[4 * LP :, at], both[: 4 * LP, at])
        returned(g).start()
        for k in range(batch):
            row = g * batch + k
            emit(me * share + row, tend[row, half])
        return carry

    lax.fori_loop(0, steps, physics, 0)

    def finish(g, carry):
        returned(g).wait_recv()
        for k in range(batch):
            row = g * batch + k
            emit((1 - me) * share + row, back[row])
        return carry

    lax.fori_loop(0, steps, finish, 0)
    over.wait_send()

    def drain(g, carry):
        returned(g).wait_send()
        return carry

    lax.fori_loop(0, steps, drain, 0)


def shards(state, winds, land_mask, first_weight, second_weight, head_weight):
    fields, levels, rows, lane = state.shape
    width = second_weight.shape[0]
    lev = lax.axis_size("lev")
    spare = LP - levels
    w1 = first_weight.reshape(9, fields, lev, levels, width).transpose(0, 2, 1, 3, 4)
    w1 = jnp.pad(w1, ((0, 0),) * 3 + ((0, spare), (0, 0))).reshape(-1, width)
    head = head_weight.transpose(0, 2, 1).reshape(2, fields, lev, levels, width)
    head = head.transpose(0, 2, 1, 3, 4)
    head = jnp.pad(head, ((0, 0),) * 3 + ((0, spare), (0, 0))).reshape(-1, width)
    inside = pl.BlockSpec(memory_space=pltpu.VMEM)
    f32, bf16 = jnp.float32, jnp.bfloat16
    share = rows // 2
    out = pl.pallas_call(
        functools.partial(kernel, (levels, rows, lane)),
        out_shape=jax.ShapeDtypeStruct((fields, levels * rows, lane), f32),
        in_specs=[inside] * 6,
        out_specs=inside,
        scratch_shapes=[
            pltpu.VMEM((rows + 2 * DEEP, 2 * LP + 16, lane), f32),
            pltpu.VMEM((rows + 2 * DEEP, 2 * LP + 16, lane), f32),
            pltpu.VMEM((rows + 2 * DEEP, 2 * LP + 32, lane), f32),
            pltpu.VMEM((2, rows + 2 * DEEP, 8, lane), f32),
            pltpu.VMEM((2, rows + 2 * DEEP, 8, lane), f32),
            pltpu.VMEM((rows + 2, 3, 2 * LP, lane), bf16),
            pltpu.VMEM((share + 2, 3, 4 * LP, lane), bf16),
            pltpu.VMEM((share, 4 * LP, lane), f32),
            pltpu.VMEM((share, 2 * LP, lane), f32),
            pltpu.VMEM((width, 9 * 4 * LP), bf16),
            pltpu.VMEM((width, width), bf16),
            pltpu.SemaphoreType.DMA((12,)),
            pltpu.SemaphoreType.DMA((12,)),
            pltpu.SemaphoreType.DMA((share // 4,)),
            pltpu.SemaphoreType.DMA((share // 4,)),
        ],
        compiler_params=pltpu.CompilerParams(
            collective_id=0, has_side_effects=True, vmem_limit_bytes=48 * 1024 * 1024
        ),
    )(
        state.reshape(fields, levels * rows, lane),
        winds.reshape(2, levels * rows, lane),
        land_mask,
        w1,
        second_weight,
        head,
    )
    return out.reshape(state.shape)


def solution(mesh):
    placed = (
        P("groups", "lev", "lat", "lon"),
        P("groups", "lev", "lat", "lon"),
        P(("groups", "lat"), "lon"),
        P(),
        P(),
        P(),
    )
    return jax.shard_map(
        shards,
        mesh=mesh,
        in_specs=placed,
        out_specs=P("groups", "lev", "lat", "lon"),
        check_vma=False,
    )
```

```python
import functools

import jax
import jax.numpy as jnp
from jax import lax
from jax.experimental import pallas as pl
from jax.experimental.pallas import tpu as pltpu
from jax.sharding import PartitionSpec as P

STEPS = 4
DEEP = STEPS + 1
LP = 32
EDGE = 8
MESH = pl.DeviceIdType.MESH


def silu(v):
    half = 0.5 * v
    return half + half * jnp.tanh(half)


def chunks():
    for c in range(LP // 8):
        yield 8 * c, LP + 8 * c, (8 * c, LP + 8 * c)
    for side in range(2):
        yield 2 * LP + 8 * side, 2 * LP + 16 + 8 * side, (2 * LP + 8 * side,)


def advance(src, winds, row, keeps):
    n = len(keeps)
    for z_at, m_at, tracers in chunks():
        zonal = [winds[row + k, z_at : z_at + 8, :] for k in range(n)]
        merid = [winds[row + k, m_at : m_at + 8, :] for k in range(n + 1)]
        for at in tracers:
            cells = [src[row - 1 + k, at : at + 8, :] for k in range(n + 2)]
            flux_y = [
                merid[k] * jnp.where(merid[k] > 0.0, cells[k], cells[k + 1])
                for k in range(n + 1)
            ]
            for k in range(n):
                here = cells[k + 1]
                lanes = here.shape[1]
                flux_x = zonal[k] * jnp.where(zonal[k] > 0.0, pltpu.roll(here, 1, 1), here)
                new = here - (pltpu.roll(flux_x, lanes - 1, 1) - flux_x)
                new = new - (flux_y[k + 1] - flux_y[k])
                yield k, at, new * keeps[k]


def kernel(
    sizes,
    state_ref, winds_ref, mask_ref, w1_ref, w2_ref, head_ref, out_ref,
    x, y, w, pack, got, cols, feats, tend, back, w1t, w2t,
    send, recv, tsend, trecv,
):
    levels, rows, lane = sizes
    lon, lat, me = lax.axis_index("lon"), lax.axis_index("lat"), lax.axis_index("lev")
    n_lon, n_lat = lax.axis_size("lon"), lax.axis_size("lat")
    share = rows // 2
    right = {"lon": lax.rem(lon + 1, n_lon)}
    left = {"lon": lax.rem(lon + n_lon - 1, n_lon)}
    north, south = {"lat": lat + 1}, {"lat": lat - 1}
    partner = {"lev": 1 - me}
    has_north, has_south = lat < n_lat - 1, lat > 0

    barrier = pltpu.get_barrier_semaphore()
    for other in (right, left, partner):
        pl.semaphore_signal(barrier, inc=1, device_id=other, device_id_type=MESH)

    @pl.when(has_north)
    def _():
        pl.semaphore_signal(barrier, inc=1, device_id=north, device_id_type=MESH)

    @pl.when(has_south)
    def _():
        pl.semaphore_signal(barrier, inc=1, device_id=south, device_id_type=MESH)

    place = lax.broadcasted_iota(jnp.int32, (8, lane), 1)
    group = place // (2 * EDGE)
    first_half = place % (2 * EDGE) < EDGE

    def tiles(ref, row):
        for f in range(2):
            for c in range(LP // 8):
                count = min(8, levels - 8 * c)
                tile = ref[f, pl.ds(row + 8 * c * rows, count, stride=rows), :]
                if count < 8:
                    tile = jnp.concatenate([tile, jnp.zeros((8 - count, lane), jnp.float32)], 0)
                yield tile

    def fill_row(row):
        tracers, winds = list(tiles(state_ref, row)), list(tiles(winds_ref, row))
        for into, values in ((x, tracers), (w, winds)):
            for c, tile in enumerate(values):
                into[DEEP + row, 8 * c : 8 * c + 8, :] = tile
        for side in range(2):
            begin = lane - EDGE if side == 0 else 0
            halves = []
            for values, half_at in ((tracers, 0), (winds, EDGE)):
                acc = jnp.zeros((8, lane), jnp.float32)
                for c, tile in enumerate(values):
                    shift = (c * 2 * EDGE + half_at - begin) % lane
                    moved = pltpu.roll(tile, shift, 1) if shift else tile
                    acc = jnp.where(group == c, moved, acc)
                halves.append(acc)
            pack[side, DEEP + row] = jnp.where(first_half, halves[0], halves[1])

    def fill(i, carry):
        for k in range(4):
            fill_row(4 * i + k)
        return carry

    lax.fori_loop(0, rows // 4, fill, 0)

    peers = 3 + jnp.where(has_north, 1, 0) + jnp.where(has_south, 1, 0)
    pl.semaphore_wait(barrier, peers)

    def remote(src, dst, k, device):
        return pltpu.make_async_remote_copy(
            src_ref=src, dst_ref=dst, send_sem=send.at[k], recv_sem=recv.at[k],
            device_id=device, device_id_type=MESH,
        )

    interior = pl.ds(DEEP, rows)
    to_right = remote(pack.at[0, interior], got.at[0, interior], 0, right)
    to_left = remote(pack.at[1, interior], got.at[1, interior], 1, left)
    low, high = pl.ds(0, DEEP), pl.ds(DEEP + rows, DEEP)
    bottom, top = pl.ds(DEEP, DEEP), pl.ds(rows, DEEP)
    main = pl.ds(0, 2 * LP)
    to_south = [
        remote(x.at[bottom, main], x.at[high, main], 2, south),
        remote(w.at[bottom, main], w.at[high, main], 3, south),
        remote(pack.at[:, bottom], pack.at[:, high], 4, south),
    ]
    to_north = [
        remote(x.at[top, main], x.at[low, main], 6, north),
        remote(w.at[top, main], w.at[low, main], 7, north),
        remote(pack.at[:, top], pack.at[:, low], 8, north),
    ]
    corner_south = remote(got.at[:, bottom], got.at[:, high], 5, south)
    corner_north = remote(got.at[:, top], got.at[:, low], 9, north)

    to_right.start()
    to_left.start()

    @pl.when(has_south)
    def _():
        for copy in to_south:
            copy.start()

    @pl.when(has_north)
    def _():
        for copy in to_north:
            copy.start()

    def clear(begin):
        for k in range(DEEP):
            x[begin + k] = jnp.zeros(x.shape[1:], jnp.float32)
            w[begin + k] = jnp.zeros(w.shape[1:], jnp.float32)
            for side in range(2):
                pack[side, begin + k] = jnp.zeros((8, lane), jnp.float32)
                got[side, begin + k] = jnp.zeros((8, lane), jnp.float32)

    @pl.when(jnp.logical_not(has_south))
    def _():
        clear(0)

    @pl.when(jnp.logical_not(has_north))
    def _():
        clear(DEEP + rows)

    w1t[...] = w1_ref[...].T
    w2t[...] = w2_ref[...].T

    to_right.wait_recv()
    to_left.wait_recv()

    @pl.when(has_south)
    def _():
        corner_south.start()

    @pl.when(has_north)
    def _():
        corner_north.start()

    def strips(row, carry):
        for side in range(2):
            if side == 0:
                outer, inner = got[0, row], pack[1, row]
            else:
                outer, inner = pack[0, row], got[1, row]
            tracer = jnp.where(first_half, outer, pltpu.roll(inner, EDGE, 1))
            wind = jnp.where(first_half, pltpu.roll(outer, lane - EDGE, 1), inner)
            swapped = pltpu.roll(wind, lane // 2, 1)
            at = 2 * LP + 8 * side
            x[row, at : at + 8, :] = tracer
            w[row, at : at + 8, :] = jnp.where(place < lane // 2, wind, swapped)
            w[row, at + 16 : at + 24, :] = jnp.where(place < lane // 2, swapped, wind)
        return carry

    def strips_four(i, carry):
        for k in range(8):
            strips(DEEP + 8 * i + k, carry)
        return carry

    lax.fori_loop(0, rows // 8, strips_four, 0)

    @pl.when(has_south)
    def _():
        for copy in to_north:
            copy.wait_recv()
        corner_north.wait_recv()

    @pl.when(has_north)
    def _():
        for copy in to_south:
            copy.wait_recv()
        corner_south.wait_recv()

    def strips_ends(k, carry):
        strips(k, carry)
        strips(DEEP + rows + k, carry)
        return carry

    lax.fori_loop(0, DEEP, strips_ends, 0)

    to_right.wait_send()
    to_left.wait_send()

    @pl.when(has_south)
    def _():
        for copy in to_south:
            copy.wait_send()
        corner_south.wait_send()

    @pl.when(has_north)
    def _():
        for copy in to_north:
            copy.wait_send()
        corner_north.wait_send()

    keep_south = jnp.where(has_south, 1.0, 0.0)
    keep_north = jnp.where(has_north, 1.0, 0.0)

    def keep(row):
        return jnp.where(
            row < DEEP, keep_south, jnp.where(row >= DEEP + rows, keep_north, 1.0)
        )

    def substep(src, dst, s):
        first = 1
        count = 2 * DEEP + rows + 1 - 2 * first - 1

        def body(i, carry):
            row = first + 8 * i
            for k, at, new in advance(src, w, row, [keep(row + k) for k in range(8)]):
                dst[row + k, at : at + 8, :] = new
            return carry

        lax.fori_loop(0, count // 8, body, 0)

    substep(x, y, 0)
    substep(y, x, 1)
    substep(x, y, 2)
    substep(y, x, 3)

    def merge_row(k):
        row = k + DEEP - 1
        west = x[row, 2 * LP : 2 * LP + 8, :]
        east = x[row, 2 * LP + 8 : 2 * LP + 16, :]
        for c in range(0, 8, 2):
            shifted = ([], [], [])
            for d in (c, c + 1):
                at = slice(8 * d, 8 * d + 8)
                from_west = pltpu.roll(west, (2 * lane - EDGE - d * 2 * EDGE) % lane, 1)
                shift = (lane - EDGE - d * 2 * EDGE) % lane
                from_east = pltpu.roll(east, shift, 1) if shift else east
                cells = jnp.where(place < STEPS, from_west, x[row, at, :])
                cells = jnp.where(place >= lane - STEPS, from_east, cells)
                y[row, at, :] = cells
                shifted[0].append(
                    pltpu.roll(jnp.where(place == lane - 1, from_west, cells), 1, 1)
                )
                shifted[1].append(cells)
                shifted[2].append(
                    pltpu.roll(jnp.where(place == 0, from_east, cells), lane - 1, 1)
                )
            for b in range(3):
                cols[k, b, 8 * c : 8 * c + 16, :] = jnp.concatenate(shifted[b], 0).astype(
                    jnp.bfloat16
                )

    def merge_from(start, count):
        def body(i, carry):
            merge_row(start + 2 * i)
            merge_row(start + 2 * i + 1)
            return carry

        lax.fori_loop(0, count // 2, body, 0)

    mine = pl.ds(me * share, share + 2)
    theirs = pl.ds((1 - me) * share, share + 2)
    half = pl.ds(me * 2 * LP, 2 * LP)
    over = remote(cols.at[theirs], feats.at[:, :, half], 10, partner)
    merge_from((1 - me) * share, share + 2)
    over.start()
    merge_from(me * (share + 2), share)
    own = pltpu.make_async_copy(cols.at[mine], feats.at[:, :, half], send.at[11])
    own.start()
    own.wait()
    over.wait_recv()

    batch = 4
    steps = share // batch

    def returned(g):
        return pltpu.make_async_remote_copy(
            src_ref=tend.at[pl.ds(g * batch, batch), pl.ds((1 - me) * 2 * LP, 2 * LP)],
            dst_ref=back.at[pl.ds(g * batch, batch)],
            send_sem=tsend.at[g], recv_sem=trecv.at[g], device_id=partner, device_id_type=MESH,
        )

    def emit(row, tendency):
        for f in range(2):
            at = slice(f * LP, f * LP + levels)
            out_ref[f, pl.ds(row, levels, stride=rows), :] = (
                y[DEEP + row, at, :] + tendency[at]
            )

    def physics(g, carry):
        features = jnp.concatenate(
            [
                feats[pl.ds(g * batch + k, 3)].reshape(9 * 4 * LP, lane)
                for k in range(batch)
            ],
            axis=1,
        )
        first = silu(
            jnp.dot(w1t[...], features, preferred_element_type=jnp.float32)
        ).astype(jnp.bfloat16)
        second = silu(
            jnp.dot(w2t[...], first, preferred_element_type=jnp.float32)
        ).astype(jnp.bfloat16)
        both = jnp.dot(head_ref[...], second, preferred_element_type=jnp.float32)
        for k in range(batch):
            row = g * batch + k
            land = mask_ref[pl.ds(me * share + row, 1), :] == 1
            at = slice(k * lane, (k + 1) * lane)
            tend[row] = jnp.where(land, both[4 * LP :, at], both[: 4 * LP, at])
        returned(g).start()
        for k in range(batch):
            row = g * batch + k
            emit(me * share + row, tend[row, half])
        return carry

    lax.fori_loop(0, steps, physics, 0, unroll=True)

    def finish(g, carry):
        returned(g).wait_recv()
        for k in range(batch):
            row = g * batch + k
            emit((1 - me) * share + row, back[row])
        return carry

    lax.fori_loop(0, steps, finish, 0)
    over.wait_send()

    def drain(g, carry):
        returned(g).wait_send()
        return carry

    lax.fori_loop(0, steps, drain, 0)


def shards(state, winds, land_mask, first_weight, second_weight, head_weight):
    fields, levels, rows, lane = state.shape
    width = second_weight.shape[0]
    lev = lax.axis_size("lev")
    spare = LP - levels
    w1 = first_weight.reshape(9, fields, lev, levels, width).transpose(0, 2, 1, 3, 4)
    w1 = jnp.pad(w1, ((0, 0),) * 3 + ((0, spare), (0, 0))).reshape(-1, width)
    head = head_weight.transpose(0, 2, 1).reshape(2, fields, lev, levels, width)
    head = head.transpose(0, 2, 1, 3, 4)
    head = jnp.pad(head, ((0, 0),) * 3 + ((0, spare), (0, 0))).reshape(-1, width)
    inside = pl.BlockSpec(memory_space=pltpu.VMEM)
    f32, bf16 = jnp.float32, jnp.bfloat16
    share = rows // 2
    out = pl.pallas_call(
        functools.partial(kernel, (levels, rows, lane)),
        out_shape=jax.ShapeDtypeStruct((fields, levels * rows, lane), f32),
        in_specs=[inside] * 6,
        out_specs=inside,
        scratch_shapes=[
            pltpu.VMEM((rows + 2 * DEEP, 2 * LP + 16, lane), f32),
            pltpu.VMEM((rows + 2 * DEEP, 2 * LP + 16, lane), f32),
            pltpu.VMEM((rows + 2 * DEEP, 2 * LP + 32, lane), f32),
            pltpu.VMEM((2, rows + 2 * DEEP, 8, lane), f32),
            pltpu.VMEM((2, rows + 2 * DEEP, 8, lane), f32),
            pltpu.VMEM((rows + 2, 3, 2 * LP, lane), bf16),
            pltpu.VMEM((share + 2, 3, 4 * LP, lane), bf16),
            pltpu.VMEM((share, 4 * LP, lane), f32),
            pltpu.VMEM((share, 2 * LP, lane), f32),
            pltpu.VMEM((width, 9 * 4 * LP), bf16),
            pltpu.VMEM((width, width), bf16),
            pltpu.SemaphoreType.DMA((12,)),
            pltpu.SemaphoreType.DMA((12,)),
            pltpu.SemaphoreType.DMA((share // 4,)),
            pltpu.SemaphoreType.DMA((share // 4,)),
        ],
        compiler_params=pltpu.CompilerParams(
            collective_id=0, has_side_effects=True, vmem_limit_bytes=48 * 1024 * 1024
        ),
    )(
        state.reshape(fields, levels * rows, lane),
        winds.reshape(2, levels * rows, lane),
        land_mask,
        w1,
        second_weight,
        head,
    )
    return out.reshape(state.shape)


def solution(mesh):
    placed = (
        P("groups", "lev", "lat", "lon"),
        P("groups", "lev", "lat", "lon"),
        P(("groups", "lat"), "lon"),
        P(),
        P(),
        P(),
    )
    return jax.shard_map(
        shards,
        mesh=mesh,
        in_specs=placed,
        out_specs=P("groups", "lev", "lat", "lon"),
        check_vma=False,
    )
```

```python
import functools

import jax
import jax.numpy as jnp
from jax import lax
from jax.experimental import pallas as pl
from jax.experimental.pallas import tpu as pltpu
from jax.sharding import PartitionSpec as P

STEPS = 4
DEEP = STEPS + 1
LP = 32
EDGE = 8
MESH = pl.DeviceIdType.MESH


def silu(v):
    half = 0.5 * v
    return half + half * jnp.tanh(half)


def chunks():
    for c in range(LP // 8):
        yield 8 * c, LP + 8 * c, (8 * c, LP + 8 * c)
    for side in range(2):
        yield 2 * LP + 8 * side, 2 * LP + 16 + 8 * side, (2 * LP + 8 * side,)


def advance(src, winds, row, keeps):
    n = len(keeps)
    for z_at, m_at, tracers in chunks():
        zonal = [winds[row + k, z_at : z_at + 8, :] for k in range(n)]
        merid = [winds[row + k, m_at : m_at + 8, :] for k in range(n + 1)]
        for at in tracers:
            cells = [src[row - 1 + k, at : at + 8, :] for k in range(n + 2)]
            flux_y = [
                merid[k] * jnp.where(merid[k] > 0.0, cells[k], cells[k + 1])
                for k in range(n + 1)
            ]
            for k in range(n):
                here = cells[k + 1]
                lanes = here.shape[1]
                flux_x = zonal[k] * jnp.where(zonal[k] > 0.0, pltpu.roll(here, 1, 1), here)
                new = here - (pltpu.roll(flux_x, lanes - 1, 1) - flux_x)
                new = new - (flux_y[k + 1] - flux_y[k])
                yield k, at, new * keeps[k]


def kernel(
    sizes,
    state_ref, winds_ref, mask_ref, w1_ref, w2_ref, head_ref, out_ref,
    x, y, w, pack, got, cols, feats, tend, back, w1t, w2t,
    send, recv, tsend, trecv,
):
    levels, rows, lane = sizes
    lon, lat, me = lax.axis_index("lon"), lax.axis_index("lat"), lax.axis_index("lev")
    n_lon, n_lat = lax.axis_size("lon"), lax.axis_size("lat")
    share = rows // 2
    right = {"lon": lax.rem(lon + 1, n_lon)}
    left = {"lon": lax.rem(lon + n_lon - 1, n_lon)}
    north, south = {"lat": lat + 1}, {"lat": lat - 1}
    partner = {"lev": 1 - me}
    has_north, has_south = lat < n_lat - 1, lat > 0

    barrier = pltpu.get_barrier_semaphore()
    for other in (right, left, partner):
        pl.semaphore_signal(barrier, inc=1, device_id=other, device_id_type=MESH)

    @pl.when(has_north)
    def _():
        pl.semaphore_signal(barrier, inc=1, device_id=north, device_id_type=MESH)

    @pl.when(has_south)
    def _():
        pl.semaphore_signal(barrier, inc=1, device_id=south, device_id_type=MESH)

    place = lax.broadcasted_iota(jnp.int32, (8, lane), 1)
    group = place // (2 * EDGE)
    first_half = place % (2 * EDGE) < EDGE

    def tiles(ref, row):
        for f in range(2):
            for c in range(LP // 8):
                count = min(8, levels - 8 * c)
                tile = ref[f, pl.ds(row + 8 * c * rows, count, stride=rows), :]
                if count < 8:
                    tile = jnp.concatenate([tile, jnp.zeros((8 - count, lane), jnp.float32)], 0)
                yield tile

    def fill_row(row):
        tracers, winds = list(tiles(state_ref, row)), list(tiles(winds_ref, row))
        for into, values in ((x, tracers), (w, winds)):
            for c, tile in enumerate(values):
                into[DEEP + row, 8 * c : 8 * c + 8, :] = tile
        for side in range(2):
            begin = lane - EDGE if side == 0 else 0
            halves = []
            for values, half_at in ((tracers, 0), (winds, EDGE)):
                acc = jnp.zeros((8, lane), jnp.float32)
                for c, tile in enumerate(values):
                    shift = (c * 2 * EDGE + half_at - begin) % lane
                    moved = pltpu.roll(tile, shift, 1) if shift else tile
                    acc = jnp.where(group == c, moved, acc)
                halves.append(acc)
            pack[side, DEEP + row] = jnp.where(first_half, halves[0], halves[1])

    def fill(i, carry):
        for k in range(4):
            fill_row(4 * i + k)
        return carry

    lax.fori_loop(0, rows // 4, fill, 0)

    peers = 3 + jnp.where(has_north, 1, 0) + jnp.where(has_south, 1, 0)
    pl.semaphore_wait(barrier, peers)

    def remote(src, dst, k, device):
        return pltpu.make_async_remote_copy(
            src_ref=src, dst_ref=dst, send_sem=send.at[k], recv_sem=recv.at[k],
            device_id=device, device_id_type=MESH,
        )

    interior = pl.ds(DEEP, rows)
    to_right = remote(pack.at[0, interior], got.at[0, interior], 0, right)
    to_left = remote(pack.at[1, interior], got.at[1, interior], 1, left)
    low, high = pl.ds(0, DEEP), pl.ds(DEEP + rows, DEEP)
    bottom, top = pl.ds(DEEP, DEEP), pl.ds(rows, DEEP)
    main = pl.ds(0, 2 * LP)
    to_south = [
        remote(x.at[bottom, main], x.at[high, main], 2, south),
        remote(w.at[bottom, main], w.at[high, main], 3, south),
        remote(pack.at[:, bottom], pack.at[:, high], 4, south),
    ]
    to_north = [
        remote(x.at[top, main], x.at[low, main], 6, north),
        remote(w.at[top, main], w.at[low, main], 7, north),
        remote(pack.at[:, top], pack.at[:, low], 8, north),
    ]
    corner_south = remote(got.at[:, bottom], got.at[:, high], 5, south)
    corner_north = remote(got.at[:, top], got.at[:, low], 9, north)

    to_right.start()
    to_left.start()

    @pl.when(has_south)
    def _():
        for copy in to_south:
            copy.start()

    @pl.when(has_north)
    def _():
        for copy in to_north:
            copy.start()

    def clear(begin):
        for k in range(DEEP):
            x[begin + k] = jnp.zeros(x.shape[1:], jnp.float32)
            w[begin + k] = jnp.zeros(w.shape[1:], jnp.float32)
            for side in range(2):
                pack[side, begin + k] = jnp.zeros((8, lane), jnp.float32)
                got[side, begin + k] = jnp.zeros((8, lane), jnp.float32)

    @pl.when(jnp.logical_not(has_south))
    def _():
        clear(0)

    @pl.when(jnp.logical_not(has_north))
    def _():
        clear(DEEP + rows)

    w1t[...] = w1_ref[...].T
    w2t[...] = w2_ref[...].T

    to_right.wait_recv()
    to_left.wait_recv()

    @pl.when(has_south)
    def _():
        corner_south.start()

    @pl.when(has_north)
    def _():
        corner_north.start()

    def strips(row, carry):
        for side in range(2):
            if side == 0:
                outer, inner = got[0, row], pack[1, row]
            else:
                outer, inner = pack[0, row], got[1, row]
            tracer = jnp.where(first_half, outer, pltpu.roll(inner, EDGE, 1))
            wind = jnp.where(first_half, pltpu.roll(outer, lane - EDGE, 1), inner)
            swapped = pltpu.roll(wind, lane // 2, 1)
            at = 2 * LP + 8 * side
            x[row, at : at + 8, :] = tracer
            w[row, at : at + 8, :] = jnp.where(place < lane // 2, wind, swapped)
            w[row, at + 16 : at + 24, :] = jnp.where(place < lane // 2, swapped, wind)
        return carry

    def strips_four(i, carry):
        for k in range(8):
            strips(DEEP + 8 * i + k, carry)
        return carry

    lax.fori_loop(0, rows // 8, strips_four, 0)

    @pl.when(has_south)
    def _():
        for copy in to_north:
            copy.wait_recv()
        corner_north.wait_recv()

    @pl.when(has_north)
    def _():
        for copy in to_south:
            copy.wait_recv()
        corner_south.wait_recv()

    def strips_ends(k, carry):
        strips(k, carry)
        strips(DEEP + rows + k, carry)
        return carry

    lax.fori_loop(0, DEEP, strips_ends, 0)

    to_right.wait_send()
    to_left.wait_send()

    @pl.when(has_south)
    def _():
        for copy in to_south:
            copy.wait_send()
        corner_south.wait_send()

    @pl.when(has_north)
    def _():
        for copy in to_north:
            copy.wait_send()
        corner_north.wait_send()

    keep_south = jnp.where(has_south, 1.0, 0.0)
    keep_north = jnp.where(has_north, 1.0, 0.0)

    def keep(row):
        return jnp.where(
            row < DEEP, keep_south, jnp.where(row >= DEEP + rows, keep_north, 1.0)
        )

    def substep(src, dst, s):
        first = 1
        count = 2 * DEEP + rows + 1 - 2 * first - 1

        def body(i, carry):
            row = first + 8 * i
            for k, at, new in advance(src, w, row, [keep(row + k) for k in range(8)]):
                dst[row + k, at : at + 8, :] = new
            return carry

        lax.fori_loop(0, count // 8, body, 0)

    substep(x, y, 0)
    substep(y, x, 1)
    substep(x, y, 2)
    substep(y, x, 3)

    def merge_row(k):
        row = k + DEEP - 1
        west = x[row, 2 * LP : 2 * LP + 8, :]
        east = x[row, 2 * LP + 8 : 2 * LP + 16, :]
        for c in range(0, 8, 2):
            shifted = ([], [], [])
            for d in (c, c + 1):
                at = slice(8 * d, 8 * d + 8)
                from_west = pltpu.roll(west, (2 * lane - EDGE - d * 2 * EDGE) % lane, 1)
                shift = (lane - EDGE - d * 2 * EDGE) % lane
                from_east = pltpu.roll(east, shift, 1) if shift else east
                cells = jnp.where(place < STEPS, from_west, x[row, at, :])
                cells = jnp.where(place >= lane - STEPS, from_east, cells)
                y[row, at, :] = cells
                shifted[0].append(
                    pltpu.roll(jnp.where(place == lane - 1, from_west, cells), 1, 1)
                )
                shifted[1].append(cells)
                shifted[2].append(
                    pltpu.roll(jnp.where(place == 0, from_east, cells), lane - 1, 1)
                )
            for b in range(3):
                cols[k, b, 8 * c : 8 * c + 16, :] = jnp.concatenate(shifted[b], 0).astype(
                    jnp.bfloat16
                )

    def merge_from(start, count, each):
        def body(i, carry):
            for k in range(each):
                merge_row(start + each * i + k)
            return carry

        lax.fori_loop(0, count // each, body, 0)

    mine = pl.ds(me * share, share + 2)
    theirs = pl.ds((1 - me) * share, share + 2)
    half = pl.ds(me * 2 * LP, 2 * LP)
    over = remote(cols.at[theirs], feats.at[:, :, half], 10, partner)
    merge_from((1 - me) * share, share + 2, 3)
    over.start()
    merge_from(me * (share + 2), share, 4)
    own = pltpu.make_async_copy(cols.at[mine], feats.at[:, :, half], send.at[11])
    own.start()
    own.wait()
    over.wait_recv()

    batch = 4
    steps = share // batch

    def returned(g):
        return pltpu.make_async_remote_copy(
            src_ref=tend.at[pl.ds(g * batch, batch), pl.ds((1 - me) * 2 * LP, 2 * LP)],
            dst_ref=back.at[pl.ds(g * batch, batch)],
            send_sem=tsend.at[g], recv_sem=trecv.at[g], device_id=partner, device_id_type=MESH,
        )

    def emit(row, tendency):
        for f in range(2):
            at = slice(f * LP, f * LP + levels)
            out_ref[f, pl.ds(row, levels, stride=rows), :] = (
                y[DEEP + row, at, :] + tendency[at]
            )

    def physics(g, carry):
        features = jnp.concatenate(
            [
                feats[pl.ds(g * batch + k, 3)].reshape(9 * 4 * LP, lane)
                for k in range(batch)
            ],
            axis=1,
        )
        first = silu(
            jnp.dot(w1t[...], features, preferred_element_type=jnp.float32)
        ).astype(jnp.bfloat16)
        second = silu(
            jnp.dot(w2t[...], first, preferred_element_type=jnp.float32)
        ).astype(jnp.bfloat16)
        both = jnp.dot(head_ref[...], second, preferred_element_type=jnp.float32)
        for k in range(batch):
            row = g * batch + k
            land = mask_ref[pl.ds(me * share + row, 1), :] == 1
            at = slice(k * lane, (k + 1) * lane)
            tend[row] = jnp.where(land, both[4 * LP :, at], both[: 4 * LP, at])
        returned(g).start()
        for k in range(batch):
            row = g * batch + k
            emit(me * share + row, tend[row, half])
        return carry

    lax.fori_loop(0, steps, physics, 0, unroll=True)

    def finish(g, carry):
        returned(g).wait_recv()
        for k in range(batch):
            row = g * batch + k
            emit((1 - me) * share + row, back[row])
        return carry

    lax.fori_loop(0, steps, finish, 0)
    over.wait_send()

    def drain(g, carry):
        returned(g).wait_send()
        return carry

    lax.fori_loop(0, steps, drain, 0)


def shards(state, winds, land_mask, first_weight, second_weight, head_weight):
    fields, levels, rows, lane = state.shape
    width = second_weight.shape[0]
    lev = lax.axis_size("lev")
    spare = LP - levels
    w1 = first_weight.reshape(9, fields, lev, levels, width).transpose(0, 2, 1, 3, 4)
    w1 = jnp.pad(w1, ((0, 0),) * 3 + ((0, spare), (0, 0))).reshape(-1, width)
    head = head_weight.transpose(0, 2, 1).reshape(2, fields, lev, levels, width)
    head = head.transpose(0, 2, 1, 3, 4)
    head = jnp.pad(head, ((0, 0),) * 3 + ((0, spare), (0, 0))).reshape(-1, width)
    inside = pl.BlockSpec(memory_space=pltpu.VMEM)
    f32, bf16 = jnp.float32, jnp.bfloat16
    share = rows // 2
    out = pl.pallas_call(
        functools.partial(kernel, (levels, rows, lane)),
        out_shape=jax.ShapeDtypeStruct((fields, levels * rows, lane), f32),
        in_specs=[inside] * 6,
        out_specs=inside,
        scratch_shapes=[
            pltpu.VMEM((rows + 2 * DEEP, 2 * LP + 16, lane), f32),
            pltpu.VMEM((rows + 2 * DEEP, 2 * LP + 16, lane), f32),
            pltpu.VMEM((rows + 2 * DEEP, 2 * LP + 32, lane), f32),
            pltpu.VMEM((2, rows + 2 * DEEP, 8, lane), f32),
            pltpu.VMEM((2, rows + 2 * DEEP, 8, lane), f32),
            pltpu.VMEM((rows + 2, 3, 2 * LP, lane), bf16),
            pltpu.VMEM((share + 2, 3, 4 * LP, lane), bf16),
            pltpu.VMEM((share, 4 * LP, lane), f32),
            pltpu.VMEM((share, 2 * LP, lane), f32),
            pltpu.VMEM((width, 9 * 4 * LP), bf16),
            pltpu.VMEM((width, width), bf16),
            pltpu.SemaphoreType.DMA((12,)),
            pltpu.SemaphoreType.DMA((12,)),
            pltpu.SemaphoreType.DMA((share // 4,)),
            pltpu.SemaphoreType.DMA((share // 4,)),
        ],
        compiler_params=pltpu.CompilerParams(
            collective_id=0, has_side_effects=True, vmem_limit_bytes=48 * 1024 * 1024
        ),
    )(
        state.reshape(fields, levels * rows, lane),
        winds.reshape(2, levels * rows, lane),
        land_mask,
        w1,
        second_weight,
        head,
    )
    return out.reshape(state.shape)


def solution(mesh):
    placed = (
        P("groups", "lev", "lat", "lon"),
        P("groups", "lev", "lat", "lon"),
        P(("groups", "lat"), "lon"),
        P(),
        P(),
        P(),
    )
    return jax.shard_map(
        shards,
        mesh=mesh,
        in_specs=placed,
        out_specs=P("groups", "lev", "lat", "lon"),
        check_vma=False,
    )
```
